32 devices in a mesh: pair: 4 (over z), tm: 8 (over y, x, core).
Axes of the slice: x: 2, y: 2, z: 4, core: 2. Of those that a mesh axis runs over, the one named last changes fastest.
Arguments:
- records: bfloat16 [256, 128, 2048], P('pair', 'tm'), may hold values from -60 to 60, as said below
- pair_list: int32 [512, 2], replicated, may hold values from 0 to 255, as said below
- sketch: float32 [16, 2048], replicated, may hold values from -6 to 6
Outputs:
- stacks: float32 [512, 2048], P('pair')
The draws below stay inside these ranges and needn't reach their ends.
Inputs may be any that keep to these rules, and one draw needn't show every extreme that they name: `pair_list`: rows p * 128 to (p + 1) * 128 - 1 name at most 12 distinct channels from any one block of channels o * 64 to (o + 1) * 64 - 1, and exactly 12 from one such block; the 128 channel slots of a pair index cycle through its listed channels, so each listed channel is used. `records`: each channel is a delayed copy of a field common to all channels plus its own noise, times a channel gain.
All inputs are finite; a program needn't handle non-finite values.
Results may differ from the reference program's by a relative error of at most 0.0041.
The reference program's roundings to bfloat16 on the way (of `white` and `cross`) count: a program that leaves them out, or rounds other values in their place, can miss the bound.
Values may be sent and summed in bfloat16 or wider, within the bound.
A program may use at most 192 MiB of HBM per device.

```python
import math
import jax
import jax.numpy as jnp
from jax import lax

SAMPLES = 2048
NF = 512
LAGS = 2048
RANK = 16
CAP = 12
CH_DEV = 64
PAIRS_DEV = 128
CHANNELS = 256
WINDOWS = 128
PAIRS = 512


def one_listing(key, n_pair):
    k_count, k_hot, k_perm, k_order = jax.random.split(key, 4)
    counts = jax.random.randint(k_count, (n_pair,), CAP // 4, CAP // 2 + 1)
    hot = jax.random.randint(k_hot, (), 0, n_pair)
    counts = jnp.where(jnp.arange(n_pair) == hot, CAP, counts)
    perms = jax.vmap(lambda k: jax.random.permutation(k, CH_DEV))(jax.random.split(k_perm, n_pair))
    chosen = (jnp.arange(n_pair)[:, None] * CH_DEV + perms[:, :CAP]).reshape(-1)
    valid = (jnp.arange(CAP)[None, :] < counts[:, None]).reshape(-1)
    order = jax.random.permutation(k_order, n_pair * CAP)
    score = jnp.where(valid, order, order + n_pair * CAP)
    listed = chosen[jnp.argsort(score, stable=True)]
    used = jnp.sum(counts)
    index = jnp.arange(PAIRS_DEV)
    first = listed[jnp.mod(2 * index, used)]
    second = listed[jnp.mod(2 * index + 1, used)]
    return jnp.stack([first, second], axis=1)


def draw_pair_list(key, part):
    n_pair = PAIRS // PAIRS_DEV
    keys = jax.random.split(jax.random.fold_in(key, 11), n_pair)
    blocks = jax.vmap(lambda k: one_listing(k, n_pair))(keys)
    return blocks.reshape(PAIRS, 2).astype(jnp.int32)


def draw_records(key, part):
    k_delay, k_field, k_noise, k_gain = jax.random.split(jax.random.fold_in(key, 23), 4)
    delays = jax.random.randint(k_delay, (CHANNELS,), 0, SAMPLES)
    field = jax.random.normal(k_field, (WINDOWS, SAMPLES), jnp.float32)
    gains = jnp.exp(jax.random.uniform(k_gain, (CHANNELS,), jnp.float32, math.log(0.3), math.log(3.0)))
    noise = jax.random.normal(k_noise, (CHANNELS, WINDOWS, SAMPLES), jnp.float32)
    strength = 0.5
    times = jnp.arange(SAMPLES).astype(jnp.int32)

    def shifted(delay):
        return jnp.take(field, jnp.mod(times - delay, SAMPLES), axis=1)
    common = lax.map(shifted, delays)
    values = gains[:, None, None] * (strength * common + noise)
    return jnp.clip(values, -60.0, 60.0).astype(jnp.bfloat16)


def centred(rng, dims, scale, most, kind=jnp.bfloat16):
    entries = jax.random.normal(rng, dims, jnp.float32) * scale
    return jnp.minimum(jnp.maximum(entries, -most), most).astype(kind)


def setup_inputs(seed: int = 0) -> dict:
    seeds = jax.random.split(jax.random.key(seed), 4)
    records = draw_records(jax.random.fold_in(seeds[3], 71), 0)
    pair_list = draw_pair_list(jax.random.fold_in(seeds[3], 71), 0)
    sketch = centred(seeds[2], (RANK, LAGS), 1.0, 6.0, jnp.float32)
    return {"records": records, "pair_list": pair_list, "sketch": sketch}


def tables():
    freq = (NF // 2 + jnp.arange(NF)).astype(jnp.int32)
    times = jnp.arange(SAMPLES).astype(jnp.int32)
    turn = jnp.mod(times[:, None] * freq[None, :], SAMPLES).astype(jnp.float32) * (2.0 * math.pi / SAMPLES)
    forward = jnp.concatenate([jnp.cos(turn), jnp.sin(turn)], axis=1).astype(jnp.bfloat16)
    shifts = (jnp.arange(LAGS) - LAGS // 2).astype(jnp.int32)
    angle = jnp.mod(freq[:, None] * shifts[None, :], SAMPLES).astype(jnp.float32) * (2.0 * math.pi / SAMPLES)
    inverse = (jnp.concatenate([jnp.cos(angle), -jnp.sin(angle)], axis=0) / math.sqrt(NF)).astype(jnp.bfloat16)
    return (forward, inverse)

def whiten(block, forward):
    spectra = jnp.dot(block.astype(jnp.float32), forward.astype(jnp.float32), preferred_element_type=jnp.float32)
    real_part = spectra[:, :NF]
    imag_part = spectra[:, NF:]
    power = real_part * real_part + imag_part * imag_part
    level = lax.optimization_barrier(jnp.mean(power, axis=1, keepdims=True))
    factor = lax.rsqrt(power + level + 1e-06)
    return jnp.concatenate([real_part * factor, imag_part * factor], axis=1).astype(jnp.bfloat16)

def correlate(first, second):
    left = first.astype(jnp.float32)
    right = second.astype(jnp.float32)
    lre, lim = (left[..., :NF], left[..., NF:])
    rre, rim = (right[..., :NF], right[..., NF:])
    return jnp.concatenate([lre * rre + lim * rim, lim * rre - lre * rim], axis=-1).astype(jnp.bfloat16)

def orthonormal(raw):
    highest = lax.Precision.HIGHEST
    gram = jnp.dot(raw, raw.T, precision=highest)
    lower = jnp.linalg.cholesky(gram)
    return lax.linalg.triangular_solve(lower, raw, left_side=True, lower=True)

def reference(records, pair_list, sketch):
    highest = lax.Precision.HIGHEST
    forward, inverse = tables()
    white = lax.map(lambda block: whiten(block, forward), records)

    def one_pair(pair):
        cross = correlate(white[pair[0]], white[pair[1]])
        lagged = jnp.dot(cross.astype(jnp.float32), inverse.astype(jnp.float32), preferred_element_type=jnp.float32)
        crossf = cross.astype(jnp.float32)
        energy = jnp.sum(crossf * crossf)
        probe = jnp.dot(lagged, sketch.T, precision=highest)
        raw = jnp.dot(probe.T, lagged, precision=highest)
        basis = orthonormal(raw)
        coeffs = jnp.dot(lagged, basis.T, precision=highest)
        total = lax.optimization_barrier(jnp.sum(coeffs, axis=0))
        power = lax.optimization_barrier(jnp.sum(coeffs * coeffs, axis=0))
        gain = power / (power + energy / (2 * NF))
        return jnp.dot(gain * total / WINDOWS, basis, precision=highest)
    return lax.map(one_pair, pair_list)
```

```python
import functools
import math

import jax
import jax.numpy as jnp
import numpy as np
from jax import lax
from jax.experimental import pallas as pl
from jax.experimental.pallas import tpu as pltpu
from jax.sharding import Mesh
from jax.sharding import PartitionSpec as P

SAMPLES = 2048
NF = 512
LAGS = 2048
RANK = 16
CAP = 12
PAIRS_DEV = 128
GROUP = 8
BF = jnp.bfloat16
F32 = jnp.float32
HIGHEST = lax.Precision.HIGHEST
VMEM = 56 * 1024 * 1024
NT = (((1,), (1,)), ((), ()))


def tables():
    freq = NF // 2 + np.arange(NF)
    scale = np.float32(2.0 * math.pi / SAMPLES)
    times = np.arange(SAMPLES)
    turn = np.mod(times[:, None] * freq[None, :], SAMPLES).astype(np.float32) * scale
    forward = np.concatenate([np.cos(turn), np.sin(turn)], axis=1).astype(jnp.bfloat16)
    shifts = np.arange(LAGS) - LAGS // 2
    angle = np.mod(freq[:, None] * shifts[None, :], SAMPLES).astype(np.float32) * scale
    inverse = (
        np.concatenate([np.cos(angle), -np.sin(angle)], axis=0) / np.float32(math.sqrt(NF))
    ).astype(jnp.bfloat16)
    wide = inverse.astype(np.float64)
    return forward, inverse, (wide @ wide.T).astype(np.float32)


def split(x):
    high = x.astype(BF)
    return high, (x - high.astype(F32)).astype(BF)


def dot(a, b, dims=(((1,), (0,)), ((), ()))):
    return lax.dot_general(a, b, dims, preferred_element_type=F32)


def params():
    return pltpu.CompilerParams(vmem_limit_bytes=VMEM)


def white_kernel(idx_ref, *refs):
    blocks, forward_ref, out_ref = refs[:CAP], refs[CAP], refs[CAP + 1]
    block = jnp.concatenate([b[0] for b in blocks], axis=0)
    spectra = dot(block, forward_ref[...])
    re, im = spectra[:, :NF], spectra[:, NF:]
    power = re * re + im * im
    level = jnp.mean(power, axis=1, keepdims=True)
    factor = lax.rsqrt(power + level + 1e-06)
    rows = block.shape[0] // CAP
    out_ref[0, :, :, :NF] = (re * factor).astype(BF).reshape(CAP, rows, NF)
    out_ref[0, :, :, NF:] = (im * factor).astype(BF).reshape(CAP, rows, NF)


def whiten(records, idx, forward):
    _, win, samples = records.shape
    n = idx.shape[0] // CAP

    def pick(k):
        return pl.BlockSpec((1, win, samples), lambda d, idx, k=k: (idx[d * CAP + k], 0, 0))

    return pl.pallas_call(
        white_kernel,
        grid_spec=pltpu.PrefetchScalarGridSpec(
            num_scalar_prefetch=1,
            grid=(n,),
            in_specs=[pick(k) for k in range(CAP)]
            + [pl.BlockSpec(forward.shape, lambda d, idx: (0, 0))],
            out_specs=pl.BlockSpec((1, CAP, win, 2 * NF), lambda d, idx: (d, 0, 0, 0)),
        ),
        out_shape=jax.ShapeDtypeStruct((n, CAP, win, 2 * NF), BF),
        compiler_params=params(),
        name="whiten",
    )(idx, *([records] * CAP), forward)


def own_block(rows, row_size, cols, col_size):
    r = lax.broadcasted_iota(jnp.int32, (rows, cols), 0) // row_size
    c = lax.broadcasted_iota(jnp.int32, (rows, cols), 1) // col_size
    return r == c


def cross_kernel(slot_ref, flat_ref, high_ref, low_ref, cross_ref, raw_ref):
    step = pl.program_id(0)
    parts, _, win, _ = flat_ref.shape
    for q in range(GROUP):
        a = slot_ref[(step * GROUP + q) * 2]
        b = slot_ref[(step * GROUP + q) * 2 + 1]
        for part in range(parts):
            left = flat_ref[part, a].astype(F32)
            right = flat_ref[part, b].astype(F32)
            lre, lim = left[:, :NF], left[:, NF:]
            rre, rim = right[:, :NF], right[:, NF:]
            rows = pl.ds((q * parts + part) * win, win)
            cross_ref[rows, :NF] = (lre * rre + lim * rim).astype(BF)
            cross_ref[rows, NF:] = (lim * rre - lre * rim).astype(BF)
    cross = cross_ref[...]
    probe = dot(high_ref[...], cross, NT) + dot(low_ref[...], cross, NT)
    mine = own_block(GROUP * RANK, RANK, GROUP * parts * win, parts * win)
    high, low = split(jnp.where(mine, probe, 0.0))
    raw_ref[...] = (dot(high, cross) + dot(low, cross)).astype(BF)


def cross_and_raw(flat, slots, high, low):
    parts, _, win, _ = flat.shape
    pairs = slots.shape[0] // 2
    rows = GROUP * parts * win
    whole = lambda x: pl.BlockSpec(x.shape, lambda i, s: (0,) * x.ndim)
    return pl.pallas_call(
        cross_kernel,
        grid_spec=pltpu.PrefetchScalarGridSpec(
            num_scalar_prefetch=1,
            grid=(pairs // GROUP,),
            in_specs=[whole(flat), whole(high), whole(low)],
            out_specs=[
                pl.BlockSpec((rows, 2 * NF), lambda i, s: (i, 0)),
                pl.BlockSpec((GROUP * RANK, 2 * NF), lambda i, s: (i, 0)),
            ],
        ),
        out_shape=[
            jax.ShapeDtypeStruct((pairs * parts * win, 2 * NF), BF),
            jax.ShapeDtypeStruct((pairs * RANK, 2 * NF), BF),
        ],
        compiler_params=params(),
        name="cross",
    )(slots, flat, high, low)


def basis_kernel(parts_ref, product_ref, basis_ref, dual_ref):
    raw = parts_ref[0].astype(F32)
    for i in range(1, parts_ref.shape[0]):
        raw = raw + parts_ref[i].astype(F32)
    n = raw.shape[0]
    pairs = n // RANK
    dual = jnp.dot(raw, product_ref[...], precision=HIGHEST, preferred_element_type=F32)
    gram = lax.dot_general(raw, dual, NT, precision=HIGHEST, preferred_element_type=F32)
    gram = jnp.where(own_block(n, RANK, n, RANK), gram, 0.0)
    row = lax.broadcasted_iota(jnp.int32, (n, n), 0)
    col = lax.broadcasted_iota(jnp.int32, (n, n), 1)
    back = jnp.where(row == col, 1.0, 0.0).astype(F32)
    order = lax.broadcasted_iota(jnp.int32, (n, 1), 0) % RANK
    scale = jnp.zeros((n, 1), F32)

    def spread(x, k):
        x = x.reshape(pairs, RANK, x.shape[-1])[:, k : k + 1, :]
        return jnp.broadcast_to(x, (pairs, RANK, x.shape[-1])).reshape(n, x.shape[-1])

    for k in range(RANK):
        column = jnp.sum(jnp.where(col % RANK == k, gram, 0.0), axis=1, keepdims=True)
        pivot = spread(column, k)
        scale = jnp.where(order == k, lax.rsqrt(pivot), scale)
        if k < RANK - 1:
            ratio = jnp.where(order > k, column / pivot, 0.0)
            gram = gram - ratio * spread(gram, k)
            back = back - ratio * spread(back, k)
    back = back * scale
    basis_ref[...] = jnp.dot(back, raw, precision=HIGHEST, preferred_element_type=F32)
    dual_ref[...] = jnp.dot(
        back, dual, precision=HIGHEST, preferred_element_type=F32
    ).astype(BF)


def orthonormal(parts, product):
    n = parts.shape[1]
    return pl.pallas_call(
        basis_kernel,
        out_shape=[
            jax.ShapeDtypeStruct((n, 2 * NF), F32),
            jax.ShapeDtypeStruct((n, 2 * NF), BF),
        ],
        compiler_params=params(),
        name="basis",
    )(parts, product)


def sums_kernel(cross_ref, dual_ref, out_ref):
    cross = cross_ref[...]
    rows = cross.shape[0]
    coeffs = dot(cross, dual_ref[...], NT)
    mine = own_block(rows, rows // GROUP, GROUP * RANK, RANK)
    coeffs = jnp.where(mine, coeffs, 0.0)
    wide = cross.astype(F32)
    energy = jnp.sum(wide * wide, axis=1, keepdims=True)
    out_ref[0, 0:1, :] = jnp.sum(coeffs, axis=0, keepdims=True)
    out_ref[0, 1:2, :] = jnp.sum(coeffs * coeffs, axis=0, keepdims=True)
    out_ref[0, 2:3, :] = jnp.sum(jnp.where(mine, energy, 0.0), axis=0, keepdims=True)


def window_sums(cross, dual):
    steps = dual.shape[0] // (GROUP * RANK)
    rows = cross.shape[0] // steps
    return pl.pallas_call(
        sums_kernel,
        grid=(steps,),
        in_specs=[
            pl.BlockSpec((rows, 2 * NF), lambda i: (i, 0)),
            pl.BlockSpec((GROUP * RANK, 2 * NF), lambda i: (i, 0)),
        ],
        out_specs=pl.BlockSpec((1, 3, GROUP * RANK), lambda i: (i, 0, 0)),
        out_shape=jax.ShapeDtypeStruct((steps, 3, GROUP * RANK), F32),
        compiler_params=params(),
        name="sums",
    )(cross, dual)


def stack_kernel(weights_ref, inverse_ref, out_ref):
    high, low = split(weights_ref[...])
    out_ref[...] = dot(high, inverse_ref[...]) + dot(low, inverse_ref[...])


def stack(weights, inverse):
    pairs = weights.shape[0]
    tile = 512
    return pl.pallas_call(
        stack_kernel,
        grid=(LAGS // tile,),
        in_specs=[
            pl.BlockSpec(weights.shape, lambda i: (0, 0)),
            pl.BlockSpec((2 * NF, tile), lambda i: (0, i)),
        ],
        out_specs=pl.BlockSpec((pairs, tile), lambda i: (0, i)),
        out_shape=jax.ShapeDtypeStruct((pairs, LAGS), F32),
        compiler_params=params(),
        name="stack",
    )(weights, inverse)


def plan(pair_list, n_pair, ch_dev, owner):
    lists = pair_list.reshape(n_pair, 2 * PAIRS_DEV)
    every = jnp.arange(n_pair * ch_dev)
    asked = jnp.any(lists[:, None, :] == every[None, :, None], axis=2)
    blocks = asked.reshape(n_pair, n_pair, ch_dev)
    before = jnp.arange(ch_dev)[None, :] < jnp.arange(ch_dev)[:, None]
    rank = jnp.sum((blocks[:, :, None, :] & before).astype(jnp.int32), axis=3)
    mine = lax.dynamic_slice_in_dim(blocks, owner, 1, 1)[:, 0]
    mine_rank = lax.dynamic_slice_in_dim(rank, owner, 1, 1)[:, 0]
    hit = mine[:, None, :] & (mine_rank[:, None, :] == jnp.arange(CAP)[None, :, None])
    idx = jnp.sum(jnp.where(hit, jnp.arange(ch_dev), 0), axis=2).reshape(-1)
    place = (rank + CAP * jnp.arange(n_pair)[None, :, None]).reshape(n_pair, -1)
    place = lax.dynamic_slice_in_dim(place, owner, 1, 0)[0]
    wanted = lax.dynamic_slice_in_dim(lists, owner, 1, 0)[0]
    slots = jnp.sum(jnp.where(wanted[:, None] == every[None, :], place[None, :], 0), axis=1)
    return idx.astype(jnp.int32), slots.astype(jnp.int32)


def local(forward, inverse, product, records, pair_list, sketch):
    n_pair = lax.axis_size("pair")
    chips = lax.axis_size("chip")
    cores = lax.axis_size("core")
    owner = lax.axis_index("pair")
    core = lax.axis_index("core")
    ch_dev, win, _ = records.shape
    half = PAIRS_DEV // cores
    idx, slots = plan(pair_list, n_pair, ch_dev, owner)
    outgoing = whiten(records, idx, forward)
    arrived = lax.all_to_all(outgoing, "pair", split_axis=0, concat_axis=0, tiled=True)
    arrived = arrived.reshape(n_pair * CAP, win, 2 * NF)
    flat = lax.all_gather(arrived, "core", axis=0)

    probe = jnp.einsum("rl,fl->rf", sketch, inverse.astype(F32), precision=HIGHEST)
    high = lax.reduce_precision(probe, 8, 7)
    low = (probe - high).astype(BF)
    high = jnp.tile(high.astype(BF), (GROUP, 1))
    low = jnp.tile(low, (GROUP, 1))
    slots = lax.dynamic_slice_in_dim(slots, core * half * 2, half * 2, 0)
    cross, raw = cross_and_raw(flat, slots, high, low)
    raw = raw.reshape(chips, half // chips * RANK, 2 * NF)
    parts = lax.all_to_all(raw, "chip", split_axis=0, concat_axis=0, tiled=True)
    basis, dual = orthonormal(parts, product)
    dual = lax.all_gather(dual, "chip", axis=0, tiled=True)
    sums = window_sums(cross, dual)
    sums = jnp.swapaxes(sums, 0, 1).reshape(3, half * RANK)
    sums = lax.psum(sums, "chip")
    own = half // chips * RANK
    sums = lax.dynamic_slice_in_dim(sums, lax.axis_index("chip") * own, own, 1)
    total, power, energy = sums[0], sums[1], sums[2]
    gain = power / (power + energy / (2 * NF))
    windows = win * chips * cores
    weights = (gain * total / windows)[:, None] * basis
    weights = jnp.sum(weights.reshape(half // chips, RANK, 2 * NF), axis=1)
    weights = lax.all_gather(weights, ("chip", "core"), axis=0)
    weights = weights.reshape(chips, cores, half // chips, 2 * NF)
    weights = jnp.swapaxes(weights, 0, 1).reshape(PAIRS_DEV, 2 * NF)
    return stack(weights, inverse)


def solution(mesh):
    n_pair, n_tm = mesh.devices.shape
    fine = Mesh(mesh.devices.reshape(n_pair, n_tm // 2, 2), ("pair", "chip", "core"))
    forward, inverse, product = tables()
    in_specs = (P("pair", ("chip", "core"), None), P(), P())

    def run(records, pair_list, sketch):
        f = functools.partial(
            local, jnp.asarray(forward), jnp.asarray(inverse), jnp.asarray(product)
        )
        return jax.shard_map(
            f, mesh=fine, in_specs=in_specs, out_specs=P("pair", None), check_vma=False
        )(records, pair_list, sketch)

    return run
```

```python
import functools
import math

import jax
import jax.numpy as jnp
import numpy as np
from jax import lax
from jax.experimental import pallas as pl
from jax.experimental.pallas import tpu as pltpu
from jax.sharding import Mesh
from jax.sharding import PartitionSpec as P

SAMPLES = 2048
NF = 512
LAGS = 2048
RANK = 16
CAP = 12
PAIRS_DEV = 128
GROUP = 8
BF = jnp.bfloat16
F32 = jnp.float32
HIGHEST = lax.Precision.HIGHEST
VMEM = 56 * 1024 * 1024
NT = (((1,), (1,)), ((), ()))


def tables():
    freq = NF // 2 + np.arange(NF)
    scale = np.float32(2.0 * math.pi / SAMPLES)
    times = np.arange(SAMPLES)
    turn = np.mod(times[:, None] * freq[None, :], SAMPLES).astype(np.float32) * scale
    forward = np.concatenate([np.cos(turn), np.sin(turn)], axis=1).astype(jnp.bfloat16)
    shifts = np.arange(LAGS) - LAGS // 2
    angle = np.mod(freq[:, None] * shifts[None, :], SAMPLES).astype(np.float32) * scale
    inverse = (
        np.concatenate([np.cos(angle), -np.sin(angle)], axis=0) / np.float32(math.sqrt(NF))
    ).astype(jnp.bfloat16)
    wide = inverse.astype(np.float64)
    return forward, inverse, (wide @ wide.T).astype(np.float32)


def split(x):
    high = x.astype(BF)
    return high, (x - high.astype(F32)).astype(BF)


def dot(a, b, dims=(((1,), (0,)), ((), ()))):
    return lax.dot_general(a, b, dims, preferred_element_type=F32)


def params():
    return pltpu.CompilerParams(vmem_limit_bytes=VMEM)


MESH = pl.DeviceIdType.MESH


def own_block(rows, row_size, cols, col_size):
    r = lax.broadcasted_iota(jnp.int32, (rows, cols), 0) // row_size
    c = lax.broadcasted_iota(jnp.int32, (rows, cols), 1) // col_size
    return r == c


def partner(me, k, n):
    out = 0
    bit = 1
    while bit < n:
        digit = (me // bit) % 2
        out = out + bit * (1 - digit if (k // bit) % 2 else digit)
        bit *= 2
    return out


def greet(others):
    barrier = pltpu.get_barrier_semaphore()
    for device in others:
        pl.semaphore_signal(barrier, inc=1, device_id=device, device_id_type=MESH)
    pl.semaphore_wait(barrier, len(others))


def send(src, dst, sems, at, device):
    copy = pltpu.make_async_remote_copy(
        src_ref=src,
        dst_ref=dst,
        send_sem=sems[0].at[at],
        recv_sem=sems[1].at[at],
        device_id=device,
        device_id_type=MESH,
    )
    copy.start()
    return copy


def white_kernel(n, idx_ref, records_ref, forward_ref, flat_ref, out_buf, zs, zr, cs, cr):
    me = lax.axis_index("pair")
    core = lax.axis_index("core")
    sibling = {"core": 1 - core}
    greet([{"pair": partner(me, k, n)} for k in range(1, n)] + [sibling])

    def whitened(d, put):
        block = jnp.concatenate([records_ref[idx_ref[d * CAP + j]] for j in range(CAP)], axis=0)
        spectra = dot(block, forward_ref[...])
        re, im = spectra[:, :NF], spectra[:, NF:]
        power = re * re + im * im
        level = jnp.mean(power, axis=1, keepdims=True)
        factor = lax.rsqrt(power + level + 1e-06)
        win = block.shape[0] // CAP
        put(0, (re * factor).astype(BF).reshape(CAP, win, NF))
        put(NF, (im * factor).astype(BF).reshape(CAP, win, NF))

    order = list(range(n // 2, n)) + list(range(1, n // 2))
    copies = {}
    for k in order:
        d = partner(me, k, n)

        def put(at, value, k=k):
            out_buf[k - 1, :, :, at : at + NF] = value

        whitened(d, put)
        copies[k] = send(out_buf.at[k - 1], flat_ref.at[core, me], (zs, zr), k - 1, {"pair": d})

    def put_own(at, value):
        flat_ref[core, me, :, :, at : at + NF] = value

    whitened(me, put_own)
    shared = [send(flat_ref.at[core, me], flat_ref.at[core, me], (cs, cr), 0, sibling)]
    for k in [*range(1, n // 2), *range(n // 2, n)]:
        copies[k].wait_recv()
        block = flat_ref.at[core, partner(me, k, n)]
        shared.append(send(block, block, (cs, cr), k, sibling))
    for k in order:
        copies[k].wait_send()
    for copy in shared:
        copy.wait()


def white_exchange(records, idx, forward):
    _, win, _ = records.shape
    n = idx.shape[0] // CAP
    vmem = pl.BlockSpec(memory_space=pltpu.VMEM)
    return pl.pallas_call(
        functools.partial(white_kernel, n),
        in_specs=[pl.BlockSpec(memory_space=pltpu.SMEM), vmem, vmem],
        out_specs=vmem,
        out_shape=jax.ShapeDtypeStruct((2, n, CAP, win, 2 * NF), BF),
        scratch_shapes=[
            pltpu.VMEM((n - 1, CAP, win, 2 * NF), BF),
            pltpu.SemaphoreType.DMA((n - 1,)),
            pltpu.SemaphoreType.DMA((n - 1,)),
            pltpu.SemaphoreType.DMA((n,)),
            pltpu.SemaphoreType.DMA((n,)),
        ],
        compiler_params=pltpu.CompilerParams(
            vmem_limit_bytes=VMEM, collective_id=0, has_side_effects=True
        ),
        name="white_exchange",
    )(idx, records, forward)


def full(a, b, dims=(((1,), (0,)), ((), ()))):
    return lax.dot_general(a, b, dims, precision=HIGHEST, preferred_element_type=F32)


def eliminate(gram):
    n = gram.shape[0]
    pairs = n // RANK
    row = lax.broadcasted_iota(jnp.int32, (n, n), 0)
    col = lax.broadcasted_iota(jnp.int32, (n, n), 1)
    gram = jnp.where(row // RANK == col // RANK, gram, 0.0)
    back = jnp.where(row == col, 1.0, 0.0).astype(F32)
    order = lax.broadcasted_iota(jnp.int32, (n, 1), 0) % RANK
    scale = jnp.zeros((n, 1), F32)

    def spread(x, k):
        x = x.reshape(pairs, RANK, x.shape[-1])[:, k : k + 1, :]
        return jnp.broadcast_to(x, (pairs, RANK, x.shape[-1])).reshape(n, x.shape[-1])

    for k in range(RANK):
        column = jnp.sum(jnp.where(col % RANK == k, gram, 0.0), axis=1, keepdims=True)
        pivot = spread(column, k)
        scale = jnp.where(order == k, lax.rsqrt(pivot), scale)
        if k < RANK - 1:
            ratio = jnp.where(order > k, column / pivot, 0.0)
            gram = gram - ratio * spread(gram, k)
            back = back - ratio * spread(back, k)
    return back * scale


def pair_kernel(
    chips, windows, slot_ref, flat_ref, high_ref, low_ref, product_ref, out_ref,
    cross_ref, raw_buf, raw_in, energy_ref, dual_ref, sums_buf, sums_in,
    rs, rr, ds, dr, ss, sr, ws, wr,
):
    me = lax.axis_index("chip")
    core = lax.axis_index("core")
    there = [partner(me, k, chips) for k in range(chips)]
    groups = sums_buf.shape[1]
    lanes = GROUP * RANK
    _, _, win, _ = flat_ref.shape
    rows = GROUP * 2 * win
    everyone = [(k, c) for k in range(chips) for c in range(2) if k or c]

    def device(k, c):
        return {"chip": there[k], "core": 1 - core if c else core}

    greet([device(k, c) for k, c in everyone])
    order = list(range(chips - 1, 0, -1))

    sent = {}
    for k in order + [0]:
        for g in range(groups):
            step = there[k] * groups + g

            @pl.loop(0, GROUP)
            def _(q, step=step):
                a = slot_ref[(step * GROUP + q) * 2]
                b = slot_ref[(step * GROUP + q) * 2 + 1]
                for part in range(2):
                    left = flat_ref[part, a].astype(F32)
                    right = flat_ref[part, b].astype(F32)
                    lre, lim = left[:, :NF], left[:, NF:]
                    rre, rim = right[:, :NF], right[:, NF:]
                    at = pl.ds(pl.multiple_of((q * 2 + part) * win, 16), win)
                    cross_ref[step, at, :NF] = (lre * rre + lim * rim).astype(BF)
                    cross_ref[step, at, NF:] = (lim * rre - lre * rim).astype(BF)

            cross = cross_ref[step]
            probe = dot(high_ref[...], cross, NT) + dot(low_ref[...], cross, NT)
            high, low = split(jnp.where(own_block(lanes, RANK, rows, 2 * win), probe, 0.0))
            raw = dot(high, cross) + dot(low, cross)
            raw_buf[k, g * lanes : (g + 1) * lanes, :] = raw.astype(BF)
            wide = cross.astype(F32)
            energy = jnp.sum(wide * wide, axis=1, keepdims=True)
            energy = jnp.where(own_block(rows, 2 * win, lanes, RANK), energy, 0.0)
            energy_ref[step] = jnp.sum(energy, axis=0, keepdims=True)
        if k:
            sent[k] = send(raw_buf.at[k], raw_in.at[k - 1], (rs, rr), k - 1, device(k, 0))

    raw = raw_buf[0].astype(F32)
    for k in order:
        sent[k].wait()
        raw = raw + raw_in[k - 1].astype(F32)
    dual = full(raw, product_ref[...])
    back = eliminate(full(raw, dual, NT))
    dual_ref[0] = full(back, dual).astype(BF)
    sent = {}
    for k in order:
        sent[k] = send(dual_ref.at[0], dual_ref.at[k], (ds, dr), k - 1, device(k, 0))

    summed = {}
    for k in [0] + order[::-1]:
        if k:
            sent[k].wait()
        for g in range(groups):
            step = there[k] * groups + g
            part = dual_ref[k, g * lanes : (g + 1) * lanes, :]
            coeffs = dot(cross_ref[step], part, NT)
            coeffs = jnp.where(own_block(rows, 2 * win, lanes, RANK), coeffs, 0.0)
            total = jnp.sum(coeffs, axis=0, keepdims=True)
            power = jnp.sum(coeffs * coeffs, axis=0, keepdims=True)
            pad = jnp.zeros((5, lanes), F32)
            sums_buf[k, g] = jnp.concatenate([total, power, energy_ref[step], pad], axis=0)
        if k:
            summed[k] = send(sums_buf.at[k], sums_in.at[k - 1], (ss, sr), k - 1, device(k, 0))
    sums = sums_buf[0]
    for k in order[::-1]:
        summed[k].wait()
        sums = sums + sums_in[k - 1]
    total, power, energy = sums[:, 0:1, :], sums[:, 1:2, :], sums[:, 2:3, :]
    weight = power / (power + energy / (2 * NF)) * total / windows
    weight = jnp.concatenate([weight[g] for g in range(groups)], axis=1)
    pairs = groups * GROUP
    weight = jnp.where(own_block(pairs, 1, pairs * RANK, RANK), weight, 0.0)
    out_ref[core, me] = full(full(weight, back), raw)
    mine = out_ref.at[core, me]
    last = [send(mine, mine, (ws, wr), 2 * k + c - 1, device(k, c)) for k, c in everyone]
    for copy in last:
        copy.wait()


def pair_weights(flat, slots, high, low, product, chips, windows):
    parts, _, win, _ = flat.shape
    pairs = slots.shape[0] // 2
    groups = pairs // chips // GROUP
    lanes = GROUP * RANK
    steps = pairs // GROUP
    vmem = pl.BlockSpec(memory_space=pltpu.VMEM)
    dma = pltpu.SemaphoreType.DMA
    return pl.pallas_call(
        functools.partial(pair_kernel, chips, windows),
        in_specs=[pl.BlockSpec(memory_space=pltpu.SMEM)] + [vmem] * 4,
        out_specs=vmem,
        out_shape=jax.ShapeDtypeStruct((2, chips, pairs // chips, 2 * NF), F32),
        scratch_shapes=[
            pltpu.VMEM((steps, GROUP * parts * win, 2 * NF), BF),
            pltpu.VMEM((chips, groups * lanes, 2 * NF), BF),
            pltpu.VMEM((chips - 1, groups * lanes, 2 * NF), BF),
            pltpu.VMEM((steps, 1, lanes), F32),
            pltpu.VMEM((chips, groups * lanes, 2 * NF), BF),
            pltpu.VMEM((chips, groups, 8, lanes), F32),
            pltpu.VMEM((chips - 1, groups, 8, lanes), F32),
        ]
        + [dma((chips - 1,))] * 6
        + [dma((2 * chips - 1,))] * 2,
        compiler_params=pltpu.CompilerParams(
            vmem_limit_bytes=VMEM, collective_id=1, has_side_effects=True
        ),
        name="pair_weights",
    )(slots, flat, high, low, product)


def stack_kernel(weights_ref, inverse_ref, out_ref):
    high, low = split(weights_ref[...])
    out_ref[...] = dot(high, inverse_ref[...]) + dot(low, inverse_ref[...])


def stack(weights, inverse):
    pairs = weights.shape[0]
    tile = 512
    return pl.pallas_call(
        stack_kernel,
        grid=(LAGS // tile,),
        in_specs=[
            pl.BlockSpec(weights.shape, lambda i: (0, 0)),
            pl.BlockSpec((2 * NF, tile), lambda i: (0, i)),
        ],
        out_specs=pl.BlockSpec((pairs, tile), lambda i: (0, i)),
        out_shape=jax.ShapeDtypeStruct((pairs, LAGS), F32),
        compiler_params=params(),
        name="stack",
    )(weights, inverse)


def plan(pair_list, n_pair, ch_dev, owner):
    lists = pair_list.reshape(n_pair, 2 * PAIRS_DEV)
    every = jnp.arange(n_pair * ch_dev)
    asked = jnp.any(lists[:, None, :] == every[None, :, None], axis=2)
    blocks = asked.reshape(n_pair, n_pair, ch_dev)
    before = jnp.arange(ch_dev)[None, :] < jnp.arange(ch_dev)[:, None]
    rank = jnp.sum((blocks[:, :, None, :] & before).astype(jnp.int32), axis=3)
    mine = lax.dynamic_slice_in_dim(blocks, owner, 1, 1)[:, 0]
    mine_rank = lax.dynamic_slice_in_dim(rank, owner, 1, 1)[:, 0]
    hit = mine[:, None, :] & (mine_rank[:, None, :] == jnp.arange(CAP)[None, :, None])
    idx = jnp.sum(jnp.where(hit, jnp.arange(ch_dev), 0), axis=2).reshape(-1)
    place = (rank + CAP * jnp.arange(n_pair)[None, :, None]).reshape(n_pair, -1)
    place = lax.dynamic_slice_in_dim(place, owner, 1, 0)[0]
    wanted = lax.dynamic_slice_in_dim(lists, owner, 1, 0)[0]
    slots = jnp.sum(jnp.where(wanted[:, None] == every[None, :], place[None, :], 0), axis=1)
    return idx.astype(jnp.int32), slots.astype(jnp.int32)


def local(forward, inverse, product, records, pair_list, sketch):
    n_pair = lax.axis_size("pair")
    chips = lax.axis_size("chip")
    cores = lax.axis_size("core")
    owner = lax.axis_index("pair")
    core = lax.axis_index("core")
    ch_dev, win, _ = records.shape
    half = PAIRS_DEV // cores
    idx, slots = plan(pair_list, n_pair, ch_dev, owner)
    flat = white_exchange(records, idx, forward)
    flat = flat.reshape(cores, n_pair * CAP, win, 2 * NF)

    probe = jnp.einsum("rl,fl->rf", sketch, inverse.astype(F32), precision=HIGHEST)
    high = lax.reduce_precision(probe, 8, 7)
    low = (probe - high).astype(BF)
    high = jnp.tile(high.astype(BF), (GROUP, 1))
    low = jnp.tile(low, (GROUP, 1))
    slots = lax.dynamic_slice_in_dim(slots, core * half * 2, half * 2, 0)
    weights = pair_weights(flat, slots, high, low, product, chips, win * chips * cores)
    return stack(weights.reshape(PAIRS_DEV, 2 * NF), inverse)


def solution(mesh):
    n_pair, n_tm = mesh.devices.shape
    fine = Mesh(mesh.devices.reshape(n_pair, n_tm // 2, 2), ("pair", "chip", "core"))
    forward, inverse, product = tables()
    in_specs = (P("pair", ("chip", "core"), None), P(), P())

    def run(records, pair_list, sketch):
        f = functools.partial(
            local, jnp.asarray(forward), jnp.asarray(inverse), jnp.asarray(product)
        )
        return jax.shard_map(
            f, mesh=fine, in_specs=in_specs, out_specs=P("pair", None), check_vma=False
        )(records, pair_list, sketch)

    return run
```

```python
import functools
import math

import jax
import jax.numpy as jnp
import numpy as np
from jax import lax
from jax.experimental import pallas as pl
from jax.experimental.pallas import tpu as pltpu
from jax.sharding import Mesh
from jax.sharding import PartitionSpec as P

SAMPLES = 2048
NF = 512
LAGS = 2048
RANK = 16
CAP = 12
PAIRS_DEV = 128
GROUP = 8
BF = jnp.bfloat16
F32 = jnp.float32
HIGHEST = lax.Precision.HIGHEST
VMEM = 56 * 1024 * 1024
NT = (((1,), (1,)), ((), ()))


def tables():
    freq = NF // 2 + np.arange(NF)
    scale = np.float32(2.0 * math.pi / SAMPLES)
    times = np.arange(SAMPLES)
    turn = np.mod(times[:, None] * freq[None, :], SAMPLES).astype(np.float32) * scale
    forward = np.concatenate([np.cos(turn), np.sin(turn)], axis=1).astype(jnp.bfloat16)
    shifts = np.arange(LAGS) - LAGS // 2
    angle = np.mod(freq[:, None] * shifts[None, :], SAMPLES).astype(np.float32) * scale
    inverse = (
        np.concatenate([np.cos(angle), -np.sin(angle)], axis=0) / np.float32(math.sqrt(NF))
    ).astype(jnp.bfloat16)
    wide = inverse.astype(np.float64)
    product = (wide @ wide.T).astype(np.float32)
    high = product.astype(jnp.bfloat16)
    low = (product - high.astype(np.float32)).astype(jnp.bfloat16)
    return forward, inverse, np.stack([high, low])


def split(x):
    high = x.astype(BF)
    return high, (x - high.astype(F32)).astype(BF)


def dot(a, b, dims=(((1,), (0,)), ((), ()))):
    return lax.dot_general(a, b, dims, preferred_element_type=F32)


def params():
    return pltpu.CompilerParams(vmem_limit_bytes=VMEM)


MESH = pl.DeviceIdType.MESH


def own_block(rows, row_size, cols, col_size):
    r = lax.broadcasted_iota(jnp.int32, (rows, cols), 0) // row_size
    c = lax.broadcasted_iota(jnp.int32, (rows, cols), 1) // col_size
    return r == c


def partner(me, k, n):
    out = 0
    bit = 1
    while bit < n:
        digit = (me // bit) % 2
        out = out + bit * (1 - digit if (k // bit) % 2 else digit)
        bit *= 2
    return out


def greet(others):
    barrier = pltpu.get_barrier_semaphore()
    for device in others:
        pl.semaphore_signal(barrier, inc=1, device_id=device, device_id_type=MESH)
    pl.semaphore_wait(barrier, len(others))


def send(src, dst, sems, at, device):
    copy = pltpu.make_async_remote_copy(
        src_ref=src,
        dst_ref=dst,
        send_sem=sems[0].at[at],
        recv_sem=sems[1].at[at],
        device_id=device,
        device_id_type=MESH,
    )
    copy.start()
    return copy


def full(a, b, dims=(((1,), (0,)), ((), ()))):
    return lax.dot_general(a, b, dims, precision=HIGHEST, preferred_element_type=F32)


def eliminate(gram):
    n = gram.shape[0]
    pairs = n // RANK
    row = lax.broadcasted_iota(jnp.int32, (n, n), 0)
    col = lax.broadcasted_iota(jnp.int32, (n, n), 1)
    gram = jnp.where(row // RANK == col // RANK, gram, 0.0)
    back = jnp.where(row == col, 1.0, 0.0).astype(F32)
    order = lax.broadcasted_iota(jnp.int32, (n, 1), 0) % RANK
    scale = jnp.zeros((n, 1), F32)

    def spread(x, k):
        x = x.reshape(pairs, RANK, x.shape[-1])[:, k : k + 1, :]
        return jnp.broadcast_to(x, (pairs, RANK, x.shape[-1])).reshape(n, x.shape[-1])

    for k in range(RANK):
        column = jnp.sum(jnp.where(col % RANK == k, gram, 0.0), axis=1, keepdims=True)
        pivot = spread(column, k)
        scale = jnp.where(order == k, lax.rsqrt(pivot), scale)
        if k < RANK - 1:
            ratio = jnp.where(order > k, column / pivot, 0.0)
            gram = gram - ratio * spread(gram, k)
            back = back - ratio * spread(back, k)
    return back * scale


def kernel(
    n, chips, windows, idx_ref, slot_ref, records_ref, forward_ref, sketch_ref, inverse_hbm,
    product_hbm, out_ref, inverse_ref, product_ref, white_buf, flat_ref, probe_ref, cross_ref,
    raw_buf, raw_in, energy_ref, dual_ref, sums_buf, sums_in,
    load, zs, zr, cs, cr, rs, rr, ds, dr, ss, sr, ws, wr,
):
    owner = lax.axis_index("pair")
    me = lax.axis_index("chip")
    core = lax.axis_index("core")
    there = [partner(me, k, chips) for k in range(chips)]
    groups = sums_buf.shape[1]
    lanes = GROUP * RANK
    win = records_ref.shape[1]
    rows = GROUP * 2 * win
    everyone = [(k, c) for k in range(chips) for c in range(2) if k or c]

    def device(k, c):
        return {"chip": there[k], "core": 1 - core if c else core}

    loads = [
        pltpu.make_async_copy(inverse_hbm, inverse_ref, load.at[0]),
        pltpu.make_async_copy(product_hbm, product_ref, load.at[1]),
    ]
    for copy in loads:
        copy.start()
    greet(
        [{"pair": partner(owner, k, n)} for k in range(1, n)] + [device(k, c) for k, c in everyone]
    )

    def slots_of(o):
        return pl.ds(pl.multiple_of(o * CAP, CAP), CAP)

    def whitened(d, put):
        block = jnp.concatenate([records_ref[idx_ref[d * CAP + j]] for j in range(CAP)], axis=0)
        spectra = dot(block, forward_ref[...])
        re, im = spectra[:, :NF], spectra[:, NF:]
        power = re * re + im * im
        level = jnp.mean(power, axis=1, keepdims=True)
        factor = lax.rsqrt(power + level + 1e-06)
        put(0, (re * factor).astype(BF).reshape(CAP, win, NF))
        put(NF, (im * factor).astype(BF).reshape(CAP, win, NF))

    far_first = list(range(n // 2, n)) + list(range(1, n // 2))
    copies = {}
    for k in far_first:
        d = partner(owner, k, n)

        def put(at, value, k=k):
            white_buf[k - 1, :, :, at : at + NF] = value

        whitened(d, put)
        copies[k] = send(
            white_buf.at[k - 1], flat_ref.at[core, slots_of(owner)], (zs, zr), k - 1, {"pair": d}
        )

    def put_own(at, value):
        flat_ref[core, slots_of(owner), :, at : at + NF] = value

    whitened(owner, put_own)
    block = flat_ref.at[core, slots_of(owner)]
    shared = [send(block, block, (cs, cr), 0, device(0, 1))]

    loads[0].wait()
    first = sketch_ref[...].astype(BF)
    second, third = split(sketch_ref[...] - first.astype(F32))
    probes = dot(jnp.concatenate([first, second, third], axis=0), inverse_ref[...], NT)
    high, low = split(probes[:RANK] + probes[RANK : 2 * RANK] + probes[2 * RANK :])
    probe_ref[0] = jnp.concatenate([high] * GROUP, axis=0)
    probe_ref[1] = jnp.concatenate([low] * GROUP, axis=0)

    for k in [*range(1, n // 2), *range(n // 2, n)]:
        copies[k].wait_recv()
        block = flat_ref.at[core, slots_of(partner(owner, k, n))]
        shared.append(send(block, block, (cs, cr), k, device(0, 1)))
    for k in far_first:
        copies[k].wait_send()
    for copy in shared:
        copy.wait()

    order = list(range(chips - 1, 0, -1))
    sent = {}
    for g in range(groups):
        for k in order + [0]:
            step = there[k] * groups + g

            @pl.loop(0, GROUP)
            def _(q, step=step):
                a = slot_ref[(step * GROUP + q) * 2]
                b = slot_ref[(step * GROUP + q) * 2 + 1]
                for part in range(2):
                    left = flat_ref[part, a].astype(F32)
                    right = flat_ref[part, b].astype(F32)
                    lre, lim = left[:, :NF], left[:, NF:]
                    rre, rim = right[:, :NF], right[:, NF:]
                    at = pl.ds(pl.multiple_of((q * 2 + part) * win, 16), win)
                    cross_ref[step, at, :NF] = (lre * rre + lim * rim).astype(BF)
                    cross_ref[step, at, NF:] = (lim * rre - lre * rim).astype(BF)

            cross = cross_ref[step]
            probe = dot(probe_ref[0], cross, NT) + dot(probe_ref[1], cross, NT)
            high, low = split(jnp.where(own_block(lanes, RANK, rows, 2 * win), probe, 0.0))
            raw_buf[k, g] = (dot(high, cross) + dot(low, cross)).astype(BF)
            if k:
                sent[k, g] = send(
                    raw_buf.at[k, g], raw_in.at[k - 1, g], (rs, rr), (k - 1, g), device(k, 0)
                )
            wide = cross.astype(F32)
            energy = jnp.sum(wide * wide, axis=1, keepdims=True)
            energy = jnp.where(own_block(rows, 2 * win, lanes, RANK), energy, 0.0)
            energy_ref[step] = jnp.sum(energy, axis=0, keepdims=True)

    relay = chips == 4 and groups == 2
    loads[1].wait()
    raws, backs, given = [], [], {}
    for g in range(groups):
        raw = raw_buf[0, g].astype(F32)
        for k in order:
            sent[k, g].wait()
            raw = raw + raw_in[k - 1, g].astype(F32)
        high, low = split(raw)
        dual = dot(high, product_ref[0]) + (dot(high, product_ref[1]) + dot(low, product_ref[0]))
        back = eliminate(full(raw, dual, NT))
        dual_ref[0, g] = full(back, dual).astype(BF)
        for k in order:
            if not (relay and k == 3):
                given[k, g] = send(
                    dual_ref.at[0, g], dual_ref.at[k, g], (ds, dr), (k - 1, g), device(k, 0)
                )
        raws.append(raw)
        backs.append(back)

    def add_up(k, g):
        step = there[k] * groups + g
        coeffs = dot(cross_ref[step], dual_ref[k, g], NT)
        coeffs = jnp.where(own_block(rows, 2 * win, lanes, RANK), coeffs, 0.0)
        total = jnp.sum(coeffs, axis=0, keepdims=True)
        power = jnp.sum(coeffs * coeffs, axis=0, keepdims=True)
        pad = jnp.zeros((5, lanes), F32)
        sums_buf[k, g] = jnp.concatenate([total, power, energy_ref[step], pad], axis=0)

    summed = {}
    if relay:
        for g, via, to in ((0, 1, 2), (1, 2, 1)):
            given[via, g].wait()
            given[3, g] = send(
                dual_ref.at[via, g], dual_ref.at[3, g], (ds, dr), (2, g), device(to, 0)
            )
    else:
        for k in order:
            for g in range(groups):
                given[k, g].wait()
    for k in [0] + order[::-1]:
        for g in range(groups):
            if relay and k and (k, g) not in ((1, 0), (2, 1)):
                given[k, g].wait()
            add_up(k, g)
        if k:
            summed[k] = send(sums_buf.at[k], sums_in.at[k - 1], (ss, sr), k - 1, device(k, 0))
    sums = sums_buf[0]
    for k in order[::-1]:
        summed[k].wait()
        sums = sums + sums_in[k - 1]
    total, power, energy = sums[:, 0:1, :], sums[:, 1:2, :], sums[:, 2:3, :]
    weight = power / (power + energy / (2 * NF)) * total / windows
    for g in range(groups):
        spread = jnp.where(own_block(GROUP, 1, lanes, RANK), weight[g], 0.0)
        out_ref[core, me, g * GROUP : (g + 1) * GROUP, :] = full(full(spread, backs[g]), raws[g])
    mine = out_ref.at[core, me]
    last = [send(mine, mine, (ws, wr), 2 * k + c - 1, device(k, c)) for k, c in everyone]
    for copy in last:
        copy.wait()


def pair_weights(records, idx, slots, sketch, held, n, chips, windows):
    forward, inverse, product = held
    _, win, _ = records.shape
    pairs = slots.shape[0] // 2
    groups = pairs // chips // GROUP
    lanes = GROUP * RANK
    steps = pairs // GROUP
    vmem = pl.BlockSpec(memory_space=pltpu.VMEM)
    smem = pl.BlockSpec(memory_space=pltpu.SMEM)
    hbm = pl.BlockSpec(memory_space=pl.ANY)
    dma = pltpu.SemaphoreType.DMA
    return pl.pallas_call(
        functools.partial(kernel, n, chips, windows),
        in_specs=[smem, smem, vmem, vmem, vmem, hbm, hbm],
        out_specs=vmem,
        out_shape=jax.ShapeDtypeStruct((2, chips, pairs // chips, 2 * NF), F32),
        scratch_shapes=[
            pltpu.VMEM(inverse.shape, BF),
            pltpu.VMEM(product.shape, BF),
            pltpu.VMEM((n - 1, CAP, win, 2 * NF), BF),
            pltpu.VMEM((2, n * CAP, win, 2 * NF), BF),
            pltpu.VMEM((2, lanes, 2 * NF), BF),
            pltpu.VMEM((steps, GROUP * 2 * win, 2 * NF), BF),
            pltpu.VMEM((chips, groups, lanes, 2 * NF), BF),
            pltpu.VMEM((chips - 1, groups, lanes, 2 * NF), BF),
            pltpu.VMEM((steps, 1, lanes), F32),
            pltpu.VMEM((chips, groups, lanes, 2 * NF), BF),
            pltpu.VMEM((chips, groups, 8, lanes), F32),
            pltpu.VMEM((chips - 1, groups, 8, lanes), F32),
            dma((2,)),
            dma((n - 1,)),
            dma((n - 1,)),
            dma((n,)),
            dma((n,)),
            dma((chips - 1, groups)),
            dma((chips - 1, groups)),
            dma((chips - 1, groups)),
            dma((chips - 1, groups)),
            dma((chips - 1,)),
            dma((chips - 1,)),
            dma((2 * chips - 1,)),
            dma((2 * chips - 1,)),
        ],
        compiler_params=pltpu.CompilerParams(
            vmem_limit_bytes=VMEM, collective_id=0, has_side_effects=True
        ),
        name="pair_weights",
    )(idx, slots, records, forward, sketch, inverse, product)


def stack_kernel(weights_ref, inverse_ref, out_ref):
    high, low = split(weights_ref[...])
    out_ref[...] = dot(high, inverse_ref[...]) + dot(low, inverse_ref[...])


def stack(weights, inverse):
    pairs = weights.shape[0]
    tile = 512
    return pl.pallas_call(
        stack_kernel,
        grid=(LAGS // tile,),
        in_specs=[
            pl.BlockSpec(weights.shape, lambda i: (0, 0)),
            pl.BlockSpec((2 * NF, tile), lambda i: (0, i)),
        ],
        out_specs=pl.BlockSpec((pairs, tile), lambda i: (0, i)),
        out_shape=jax.ShapeDtypeStruct((pairs, LAGS), F32),
        compiler_params=params(),
        name="stack",
    )(weights, inverse)


def plan(pair_list, n_pair, ch_dev, owner):
    lists = pair_list.reshape(n_pair, 2 * PAIRS_DEV)
    every = jnp.arange(n_pair * ch_dev)
    asked = jnp.any(lists[:, None, :] == every[None, :, None], axis=2)
    blocks = asked.reshape(n_pair, n_pair, ch_dev)
    before = jnp.arange(ch_dev)[None, :] < jnp.arange(ch_dev)[:, None]
    rank = jnp.sum((blocks[:, :, None, :] & before).astype(jnp.int32), axis=3)
    mine = lax.dynamic_slice_in_dim(blocks, owner, 1, 1)[:, 0]
    mine_rank = lax.dynamic_slice_in_dim(rank, owner, 1, 1)[:, 0]
    hit = mine[:, None, :] & (mine_rank[:, None, :] == jnp.arange(CAP)[None, :, None])
    idx = jnp.sum(jnp.where(hit, jnp.arange(ch_dev), 0), axis=2).reshape(-1)
    place = (rank + CAP * jnp.arange(n_pair)[None, :, None]).reshape(n_pair, -1)
    place = lax.dynamic_slice_in_dim(place, owner, 1, 0)[0]
    wanted = lax.dynamic_slice_in_dim(lists, owner, 1, 0)[0]
    slots = jnp.sum(jnp.where(wanted[:, None] == every[None, :], place[None, :], 0), axis=1)
    return idx.astype(jnp.int32), slots.astype(jnp.int32)


def local(forward, inverse, product, records, pair_list, sketch):
    n_pair = lax.axis_size("pair")
    chips = lax.axis_size("chip")
    cores = lax.axis_size("core")
    owner = lax.axis_index("pair")
    core = lax.axis_index("core")
    ch_dev, win, _ = records.shape
    half = PAIRS_DEV // cores
    idx, slots = plan(pair_list, n_pair, ch_dev, owner)
    slots = lax.dynamic_slice_in_dim(slots, core * half * 2, half * 2, 0)
    held = (forward, inverse, product)
    windows = win * chips * cores
    weights = pair_weights(records, idx, slots, sketch, held, n_pair, chips, windows)
    return stack(weights.reshape(PAIRS_DEV, 2 * NF), inverse)


def solution(mesh):
    n_pair, n_tm = mesh.devices.shape
    fine = Mesh(mesh.devices.reshape(n_pair, n_tm // 2, 2), ("pair", "chip", "core"))
    forward, inverse, product = tables()
    in_specs = (P("pair", ("chip", "core"), None), P(), P())

    def run(records, pair_list, sketch):
        f = functools.partial(
            local, jnp.asarray(forward), jnp.asarray(inverse), jnp.asarray(product)
        )
        return jax.shard_map(
            f, mesh=fine, in_specs=in_specs, out_specs=P("pair", None), check_vma=False
        )(records, pair_list, sketch)

    return run
```

```python
import functools
import math

import jax
import jax.numpy as jnp
import numpy as np
from jax import lax
from jax.experimental import pallas as pl
from jax.experimental.pallas import tpu as pltpu
from jax.sharding import Mesh
from jax.sharding import PartitionSpec as P

SAMPLES = 2048
NF = 512
LAGS = 2048
RANK = 16
CAP = 12
PAIRS_DEV = 128
GROUP = 8
BF = jnp.bfloat16
F32 = jnp.float32
HIGHEST = lax.Precision.HIGHEST
VMEM = 56 * 1024 * 1024
NT = (((1,), (1,)), ((), ()))


def tables():
    freq = NF // 2 + np.arange(NF)
    scale = np.float32(2.0 * math.pi / SAMPLES)
    times = np.arange(SAMPLES)
    turn = np.mod(times[:, None] * freq[None, :], SAMPLES).astype(np.float32) * scale
    forward = np.concatenate([np.cos(turn), np.sin(turn)], axis=1).astype(jnp.bfloat16)
    shifts = np.arange(LAGS) - LAGS // 2
    angle = np.mod(freq[:, None] * shifts[None, :], SAMPLES).astype(np.float32) * scale
    inverse = (
        np.concatenate([np.cos(angle), -np.sin(angle)], axis=0) / np.float32(math.sqrt(NF))
    ).astype(jnp.bfloat16)
    wide = inverse.astype(np.float64)
    product = (wide @ wide.T).astype(np.float32)
    high = product.astype(jnp.bfloat16)
    low = (product - high.astype(np.float32)).astype(jnp.bfloat16)
    return forward, inverse, np.stack([high, low])


def split(x):
    high = x.astype(BF)
    return high, (x - high.astype(F32)).astype(BF)


def dot(a, b, dims=(((1,), (0,)), ((), ()))):
    return lax.dot_general(a, b, dims, preferred_element_type=F32)


def params():
    return pltpu.CompilerParams(vmem_limit_bytes=VMEM)


MESH = pl.DeviceIdType.MESH


def own_block(rows, row_size, cols, col_size):
    r = lax.broadcasted_iota(jnp.int32, (rows, cols), 0) // row_size
    c = lax.broadcasted_iota(jnp.int32, (rows, cols), 1) // col_size
    return r == c


def partner(me, k, n):
    out = 0
    bit = 1
    while bit < n:
        digit = (me // bit) % 2
        out = out + bit * (1 - digit if (k // bit) % 2 else digit)
        bit *= 2
    return out


def greet(others):
    barrier = pltpu.get_barrier_semaphore()
    for device in others:
        pl.semaphore_signal(barrier, inc=1, device_id=device, device_id_type=MESH)
    pl.semaphore_wait(barrier, len(others))


def send(src, dst, sems, at, device):
    copy = pltpu.make_async_remote_copy(
        src_ref=src,
        dst_ref=dst,
        send_sem=sems[0].at[at],
        recv_sem=sems[1].at[at],
        device_id=device,
        device_id_type=MESH,
    )
    copy.start()
    return copy


def full(a, b, dims=(((1,), (0,)), ((), ()))):
    return lax.dot_general(a, b, dims, precision=HIGHEST, preferred_element_type=F32)


def eliminate(gram):
    n = gram.shape[0]
    pairs = n // RANK
    row = lax.broadcasted_iota(jnp.int32, (n, n), 0)
    col = lax.broadcasted_iota(jnp.int32, (n, n), 1)
    gram = jnp.where(row // RANK == col // RANK, gram, 0.0)
    back = jnp.where(row == col, 1.0, 0.0).astype(F32)
    order = lax.broadcasted_iota(jnp.int32, (n, 1), 0) % RANK
    scale = jnp.zeros((n, 1), F32)

    def spread(x, k):
        x = x.reshape(pairs, RANK, x.shape[-1])[:, k : k + 1, :]
        return jnp.broadcast_to(x, (pairs, RANK, x.shape[-1])).reshape(n, x.shape[-1])

    for k in range(RANK):
        column = jnp.sum(jnp.where(col % RANK == k, gram, 0.0), axis=1, keepdims=True)
        pivot = spread(column, k)
        scale = jnp.where(order == k, lax.rsqrt(pivot), scale)
        if k < RANK - 1:
            ratio = jnp.where(order > k, column / pivot, 0.0)
            gram = gram - ratio * spread(gram, k)
            back = back - ratio * spread(back, k)
    return back * scale


def kernel(
    n, chips, windows, idx_ref, slot_ref, sketch_ref, records_hbm, forward_hbm, inverse_hbm,
    product_hbm, out_ref, records_ref, forward_ref, inverse_ref, product_ref, share_ref, white_buf, flat_ref, probe_ref, cross_ref,
    raw_buf, raw_in, energy_ref, dual_ref, sums_buf, sums_in,
    load, zs, zr, cs, cr, rs, rr, ds, dr, ss, sr, ws, wr,
):
    owner = lax.axis_index("pair")
    me = lax.axis_index("chip")
    core = lax.axis_index("core")
    there = [partner(me, k, chips) for k in range(chips)]
    groups = sums_buf.shape[1]
    lanes = GROUP * RANK
    win = records_ref.shape[1]
    rows = GROUP * 2 * win
    everyone = [(k, c) for k in range(chips) for c in range(2) if k or c]

    def device(k, c):
        return {"chip": there[k], "core": 1 - core if c else core}

    loads = [
        pltpu.make_async_copy(forward_hbm, forward_ref, load.at[0]),
        pltpu.make_async_copy(records_hbm, records_ref, load.at[1]),
        pltpu.make_async_copy(inverse_hbm, inverse_ref, load.at[2]),
        pltpu.make_async_copy(product_hbm, product_ref, load.at[3]),
    ]
    for copy in loads:
        copy.start()
    greet(
        [{"pair": partner(owner, k, n)} for k in range(1, n)] + [device(k, c) for k, c in everyone]
    )

    loads[0].wait()
    loads[1].wait()

    def slots_of(o):
        return pl.ds(pl.multiple_of(o * CAP, CAP), CAP)

    def whitened(d, put):
        block = jnp.concatenate([records_ref[idx_ref[d * CAP + j]] for j in range(CAP)], axis=0)
        spectra = dot(block, forward_ref[...])
        re, im = spectra[:, :NF], spectra[:, NF:]
        power = re * re + im * im
        level = jnp.mean(power, axis=1, keepdims=True)
        factor = lax.rsqrt(power + level + 1e-06)
        put(0, (re * factor).astype(BF).reshape(CAP, win, NF))
        put(NF, (im * factor).astype(BF).reshape(CAP, win, NF))

    far_first = list(range(n // 2, n)) + list(range(1, n // 2))
    copies = {}
    for k in far_first:
        d = partner(owner, k, n)

        def put(at, value, k=k):
            white_buf[k - 1, :, :, at : at + NF] = value

        whitened(d, put)
        copies[k] = send(
            white_buf.at[k - 1], flat_ref.at[core, slots_of(owner)], (zs, zr), k - 1, {"pair": d}
        )

    def put_own(at, value):
        flat_ref[core, slots_of(owner), :, at : at + NF] = value

    whitened(owner, put_own)
    block = flat_ref.at[core, slots_of(owner)]
    shared = [send(block, block, (cs, cr), 0, device(0, 1))]

    loads[2].wait()
    first = sketch_ref[...].astype(BF)
    second, third = split(sketch_ref[...] - first.astype(F32))
    probes = dot(jnp.concatenate([first, second, third], axis=0), inverse_ref[...], NT)
    high, low = split(probes[:RANK] + probes[RANK : 2 * RANK] + probes[2 * RANK :])
    probe_ref[0] = jnp.concatenate([high] * GROUP, axis=0)
    probe_ref[1] = jnp.concatenate([low] * GROUP, axis=0)

    for k in [*range(1, n // 2), *range(n // 2, n)]:
        copies[k].wait_recv()
        block = flat_ref.at[core, slots_of(partner(owner, k, n))]
        shared.append(send(block, block, (cs, cr), k, device(0, 1)))
    for k in far_first:
        copies[k].wait_send()
    for copy in shared:
        copy.wait()

    order = list(range(chips - 1, 0, -1))
    sent = {}
    for g in range(groups):
        for k in order + [0]:
            step = there[k] * groups + g

            @pl.loop(0, GROUP)
            def _(q, step=step):
                a = slot_ref[(step * GROUP + q) * 2]
                b = slot_ref[(step * GROUP + q) * 2 + 1]
                for part in range(2):
                    left = flat_ref[part, a].astype(F32)
                    right = flat_ref[part, b].astype(F32)
                    lre, lim = left[:, :NF], left[:, NF:]
                    rre, rim = right[:, :NF], right[:, NF:]
                    at = pl.ds(pl.multiple_of((q * 2 + part) * win, 16), win)
                    cross_ref[step, at, :NF] = (lre * rre + lim * rim).astype(BF)
                    cross_ref[step, at, NF:] = (lim * rre - lre * rim).astype(BF)

            cross = cross_ref[step]
            probe = dot(probe_ref[0], cross, NT) + dot(probe_ref[1], cross, NT)
            high, low = split(jnp.where(own_block(lanes, RANK, rows, 2 * win), probe, 0.0))
            raw_buf[k, g] = (dot(high, cross) + dot(low, cross)).astype(BF)
            if k:
                sent[k, g] = send(
                    raw_buf.at[k, g], raw_in.at[k - 1, g], (rs, rr), (k - 1, g), device(k, 0)
                )
            wide = cross.astype(F32)
            energy = jnp.sum(wide * wide, axis=1, keepdims=True)
            energy = jnp.where(own_block(rows, 2 * win, lanes, RANK), energy, 0.0)
            energy_ref[step] = jnp.sum(energy, axis=0, keepdims=True)

    relay = chips == 4 and groups == 2
    loads[3].wait()
    raws, backs, given = [], [], {}
    for g in range(groups):
        raw = raw_buf[0, g].astype(F32)
        for k in order:
            sent[k, g].wait()
            raw = raw + raw_in[k - 1, g].astype(F32)
        high, low = split(raw)
        dual = dot(high, product_ref[0]) + (dot(high, product_ref[1]) + dot(low, product_ref[0]))
        back = eliminate(full(raw, dual, NT))
        dual_ref[0, g] = full(back, dual).astype(BF)
        for k in order:
            if not (relay and k == 3):
                given[k, g] = send(
                    dual_ref.at[0, g], dual_ref.at[k, g], (ds, dr), (k - 1, g), device(k, 0)
                )
        raws.append(raw)
        backs.append(back)

    def add_up(k, g):
        step = there[k] * groups + g
        coeffs = dot(cross_ref[step], dual_ref[k, g], NT)
        coeffs = jnp.where(own_block(rows, 2 * win, lanes, RANK), coeffs, 0.0)
        total = jnp.sum(coeffs, axis=0, keepdims=True)
        power = jnp.sum(coeffs * coeffs, axis=0, keepdims=True)
        pad = jnp.zeros((5, lanes), F32)
        sums_buf[k, g] = jnp.concatenate([total, power, energy_ref[step], pad], axis=0)

    summed = {}
    if relay:
        for g, via, to in ((0, 1, 2), (1, 2, 1)):
            given[via, g].wait()
            given[3, g] = send(
                dual_ref.at[via, g], dual_ref.at[3, g], (ds, dr), (2, g), device(to, 0)
            )
    else:
        for k in order:
            for g in range(groups):
                given[k, g].wait()
    for k in [0] + order[::-1]:
        for g in range(groups):
            if relay and k and (k, g) not in ((1, 0), (2, 1)):
                given[k, g].wait()
            add_up(k, g)
        if k:
            summed[k] = send(sums_buf.at[k], sums_in.at[k - 1], (ss, sr), k - 1, device(k, 0))
    sums = sums_buf[0]
    for k in order[::-1]:
        summed[k].wait()
        sums = sums + sums_in[k - 1]
    total, power, energy = sums[:, 0:1, :], sums[:, 1:2, :], sums[:, 2:3, :]
    weight = power / (power + energy / (2 * NF)) * total / windows
    mixed = []
    for g in range(groups):
        spread = jnp.where(own_block(GROUP, 1, lanes, RANK), weight[g], 0.0)
        mixed.append(full(full(spread, backs[g]), raws[g]))
    share_ref[core, me] = jnp.concatenate(mixed, axis=0).astype(share_ref.dtype)
    mine = share_ref.at[core, me]
    last = [send(mine, mine, (ws, wr), 2 * k + c - 1, device(k, c)) for k, c in everyone]
    for copy in last:
        copy.wait()

    weights = share_ref[...].reshape(PAIRS_DEV, 2 * NF)
    terms = [weights] if weights.dtype == BF else split(weights)
    for at in range(0, LAGS, 512):
        tile = inverse_ref[:, at : at + 512]
        out_ref[:, at : at + 512] = sum(dot(term, tile) for term in terms)


def pair_stacks(records, idx, slots, sketch, held, n, chips, windows):
    forward, inverse, product = held
    _, win, _ = records.shape
    pairs = slots.shape[0] // 2
    groups = pairs // chips // GROUP
    lanes = GROUP * RANK
    steps = pairs // GROUP
    own = pairs // chips
    vmem = pl.BlockSpec(memory_space=pltpu.VMEM)
    smem = pl.BlockSpec(memory_space=pltpu.SMEM)
    hbm = pl.BlockSpec(memory_space=pl.ANY)
    dma = pltpu.SemaphoreType.DMA
    return pl.pallas_call(
        functools.partial(kernel, n, chips, windows),
        in_specs=[smem, smem, vmem, hbm, hbm, hbm, hbm],
        out_specs=vmem,
        out_shape=jax.ShapeDtypeStruct((2 * pairs, LAGS), F32),
        scratch_shapes=[
            pltpu.VMEM(records.shape, BF),
            pltpu.VMEM(forward.shape, BF),
            pltpu.VMEM(inverse.shape, BF),
            pltpu.VMEM(product.shape, BF),
            pltpu.VMEM((2, chips, own, 2 * NF), BF if own % 16 == 0 else F32),
            pltpu.VMEM((n - 1, CAP, win, 2 * NF), BF),
            pltpu.VMEM((2, n * CAP, win, 2 * NF), BF),
            pltpu.VMEM((2, lanes, 2 * NF), BF),
            pltpu.VMEM((steps, GROUP * 2 * win, 2 * NF), BF),
            pltpu.VMEM((chips, groups, lanes, 2 * NF), BF),
            pltpu.VMEM((chips - 1, groups, lanes, 2 * NF), BF),
            pltpu.VMEM((steps, 1, lanes), F32),
            pltpu.VMEM((chips, groups, lanes, 2 * NF), BF),
            pltpu.VMEM((chips, groups, 8, lanes), F32),
            pltpu.VMEM((chips - 1, groups, 8, lanes), F32),
            dma((4,)),
            dma((n - 1,)),
            dma((n - 1,)),
            dma((n,)),
            dma((n,)),
            dma((chips - 1, groups)),
            dma((chips - 1, groups)),
            dma((chips - 1, groups)),
            dma((chips - 1, groups)),
            dma((chips - 1,)),
            dma((chips - 1,)),
            dma((2 * chips - 1,)),
            dma((2 * chips - 1,)),
        ],
        compiler_params=pltpu.CompilerParams(
            vmem_limit_bytes=VMEM, collective_id=0, has_side_effects=True
        ),
        name="pair_stacks",
    )(idx, slots, sketch, records, forward, inverse, product)


def plan(pair_list, n_pair, ch_dev, owner):
    lists = pair_list.reshape(n_pair, 2 * PAIRS_DEV)
    every = jnp.arange(n_pair * ch_dev)
    asked = jnp.any(lists[:, None, :] == every[None, :, None], axis=2)
    blocks = asked.reshape(n_pair, n_pair, ch_dev)
    before = jnp.arange(ch_dev)[None, :] < jnp.arange(ch_dev)[:, None]
    rank = jnp.sum((blocks[:, :, None, :] & before).astype(jnp.int32), axis=3)
    mine = lax.dynamic_slice_in_dim(blocks, owner, 1, 1)[:, 0]
    mine_rank = lax.dynamic_slice_in_dim(rank, owner, 1, 1)[:, 0]
    hit = mine[:, None, :] & (mine_rank[:, None, :] == jnp.arange(CAP)[None, :, None])
    idx = jnp.sum(jnp.where(hit, jnp.arange(ch_dev), 0), axis=2).reshape(-1)
    place = (rank + CAP * jnp.arange(n_pair)[None, :, None]).reshape(n_pair, -1)
    place = lax.dynamic_slice_in_dim(place, owner, 1, 0)[0]
    wanted = lax.dynamic_slice_in_dim(lists, owner, 1, 0)[0]
    slots = jnp.sum(jnp.where(wanted[:, None] == every[None, :], place[None, :], 0), axis=1)
    return idx.astype(jnp.int32), slots.astype(jnp.int32)


def local(forward, inverse, product, records, pair_list, sketch):
    n_pair = lax.axis_size("pair")
    chips = lax.axis_size("chip")
    cores = lax.axis_size("core")
    owner = lax.axis_index("pair")
    core = lax.axis_index("core")
    ch_dev, win, _ = records.shape
    half = PAIRS_DEV // cores
    idx, slots = plan(pair_list, n_pair, ch_dev, owner)
    slots = lax.dynamic_slice_in_dim(slots, core * half * 2, half * 2, 0)
    held = (forward, inverse, product)
    windows = win * chips * cores
    return pair_stacks(records, idx, slots, sketch, held, n_pair, chips, windows)


def solution(mesh):
    n_pair, n_tm = mesh.devices.shape
    fine = Mesh(mesh.devices.reshape(n_pair, n_tm // 2, 2), ("pair", "chip", "core"))
    forward, inverse, product = tables()
    in_specs = (P("pair", ("chip", "core"), None), P(), P())

    def run(records, pair_list, sketch):
        f = functools.partial(
            local, jnp.asarray(forward), jnp.asarray(inverse), jnp.asarray(product)
        )
        return jax.shard_map(
            f, mesh=fine, in_specs=in_specs, out_specs=P("pair", None), check_vma=False
        )(records, pair_list, sketch)

    return run
```

```python
import functools
import math

import jax
import jax.numpy as jnp
import numpy as np
from jax import lax
from jax.experimental import pallas as pl
from jax.experimental.pallas import tpu as pltpu
from jax.sharding import Mesh
from jax.sharding import PartitionSpec as P

SAMPLES = 2048
NF = 512
LAGS = 2048
RANK = 16
CAP = 12
PAIRS_DEV = 128
GROUP = 8
BF = jnp.bfloat16
F32 = jnp.float32
HIGHEST = lax.Precision.HIGHEST
VMEM = 56 * 1024 * 1024
NT = (((1,), (1,)), ((), ()))


def tables():
    freq = NF // 2 + np.arange(NF)
    scale = np.float32(2.0 * math.pi / SAMPLES)
    times = np.arange(SAMPLES)
    turn = np.mod(times[:, None] * freq[None, :], SAMPLES).astype(np.float32) * scale
    forward = np.concatenate([np.cos(turn), np.sin(turn)], axis=1).astype(jnp.bfloat16)
    shifts = np.arange(LAGS) - LAGS // 2
    angle = np.mod(freq[:, None] * shifts[None, :], SAMPLES).astype(np.float32) * scale
    inverse = (
        np.concatenate([np.cos(angle), -np.sin(angle)], axis=0) / np.float32(math.sqrt(NF))
    ).astype(jnp.bfloat16)
    wide = inverse.astype(np.float64)
    product = (wide @ wide.T).astype(np.float32)
    high = product.astype(jnp.bfloat16)
    low = (product - high.astype(np.float32)).astype(jnp.bfloat16)
    return forward, inverse, np.stack([high, low])


def split(x):
    high = x.astype(BF)
    return high, (x - high.astype(F32)).astype(BF)


def dot(a, b, dims=(((1,), (0,)), ((), ()))):
    return lax.dot_general(a, b, dims, preferred_element_type=F32)


def params():
    return pltpu.CompilerParams(vmem_limit_bytes=VMEM)


MESH = pl.DeviceIdType.MESH


def own_block(rows, row_size, cols, col_size):
    r = lax.broadcasted_iota(jnp.int32, (rows, cols), 0) // row_size
    c = lax.broadcasted_iota(jnp.int32, (rows, cols), 1) // col_size
    return r == c


def partner(me, k, n):
    out = 0
    bit = 1
    while bit < n:
        digit = (me // bit) % 2
        out = out + bit * (1 - digit if (k // bit) % 2 else digit)
        bit *= 2
    return out


def greet(others):
    barrier = pltpu.get_barrier_semaphore()
    for device in others:
        pl.semaphore_signal(barrier, inc=1, device_id=device, device_id_type=MESH)
    pl.semaphore_wait(barrier, len(others))


def send(src, dst, sems, at, device):
    copy = pltpu.make_async_remote_copy(
        src_ref=src,
        dst_ref=dst,
        send_sem=sems[0].at[at],
        recv_sem=sems[1].at[at],
        device_id=device,
        device_id_type=MESH,
    )
    copy.start()
    return copy


def full(a, b, dims=(((1,), (0,)), ((), ()))):
    return lax.dot_general(a, b, dims, precision=HIGHEST, preferred_element_type=F32)


def eliminate(gram):
    n = gram.shape[0]
    pairs = n // RANK
    row = lax.broadcasted_iota(jnp.int32, (n, n), 0)
    col = lax.broadcasted_iota(jnp.int32, (n, n), 1)
    gram = jnp.where(row // RANK == col // RANK, gram, 0.0)
    back = jnp.where(row == col, 1.0, 0.0).astype(F32)
    order = lax.broadcasted_iota(jnp.int32, (n, 1), 0) % RANK
    scale = jnp.zeros((n, 1), F32)

    def spread(x, k):
        x = x.reshape(pairs, RANK, x.shape[-1])[:, k : k + 1, :]
        return jnp.broadcast_to(x, (pairs, RANK, x.shape[-1])).reshape(n, x.shape[-1])

    for k in range(RANK):
        column = jnp.sum(jnp.where(col % RANK == k, gram, 0.0), axis=1, keepdims=True)
        pivot = spread(column, k)
        scale = jnp.where(order == k, lax.rsqrt(pivot), scale)
        if k < RANK - 1:
            ratio = jnp.where(order > k, column / pivot, 0.0)
            gram = gram - ratio * spread(gram, k)
            back = back - ratio * spread(back, k)
    return back * scale


def kernel(
    n, chips, windows, idx_ref, slot_ref, sketch_ref, records_hbm, forward_hbm, inverse_hbm,
    product_hbm, out_ref, records_ref, forward_ref, inverse_ref, product_ref, share_ref, white_buf, flat_ref, probe_ref, cross_ref,
    raw_buf, raw_in, energy_ref, dual_ref, sums_buf, sums_in,
    load, zs, zr, cs, cr, rs, rr, ds, dr, ss, sr, ws, wr,
):
    owner = lax.axis_index("pair")
    me = lax.axis_index("chip")
    core = lax.axis_index("core")
    there = [partner(me, k, chips) for k in range(chips)]
    groups = sums_buf.shape[1]
    lanes = GROUP * RANK
    win = records_ref.shape[1]
    rows = GROUP * 2 * win
    first_pair = core * (slot_ref.shape[0] // 4)
    everyone = [(k, c) for k in range(chips) for c in range(2) if k or c]

    def device(k, c):
        return {"chip": there[k], "core": 1 - core if c else core}

    loads = [
        pltpu.make_async_copy(forward_hbm, forward_ref, load.at[0]),
        pltpu.make_async_copy(records_hbm, records_ref, load.at[1]),
        pltpu.make_async_copy(inverse_hbm, inverse_ref, load.at[2]),
        pltpu.make_async_copy(product_hbm, product_ref, load.at[3]),
    ]
    for copy in loads:
        copy.start()
    greet(
        [{"pair": partner(owner, k, n)} for k in range(1, n)] + [device(k, c) for k, c in everyone]
    )

    loads[0].wait()
    loads[1].wait()

    def slots_of(o):
        return pl.ds(pl.multiple_of(o * CAP, CAP), CAP)

    def whitened(d, put):
        block = jnp.concatenate([records_ref[idx_ref[d, j]] for j in range(CAP)], axis=0)
        spectra = dot(block, forward_ref[...])
        re, im = spectra[:, :NF], spectra[:, NF:]
        power = re * re + im * im
        level = jnp.mean(power, axis=1, keepdims=True)
        factor = lax.rsqrt(power + level + 1e-06)
        put(0, (re * factor).astype(BF).reshape(CAP, win, NF))
        put(NF, (im * factor).astype(BF).reshape(CAP, win, NF))

    far_first = list(range(n // 2, n)) + list(range(1, n // 2))
    copies = {}
    for k in far_first:
        d = partner(owner, k, n)

        def put(at, value, k=k):
            white_buf[k - 1, :, :, at : at + NF] = value

        whitened(d, put)
        copies[k] = send(
            white_buf.at[k - 1], flat_ref.at[core, slots_of(owner)], (zs, zr), k - 1, {"pair": d}
        )

    def put_own(at, value):
        flat_ref[core, slots_of(owner), :, at : at + NF] = value

    whitened(owner, put_own)
    block = flat_ref.at[core, slots_of(owner)]
    shared = [send(block, block, (cs, cr), 0, device(0, 1))]

    loads[2].wait()
    first = sketch_ref[...].astype(BF)
    second, third = split(sketch_ref[...] - first.astype(F32))
    probes = dot(jnp.concatenate([first, second, third], axis=0), inverse_ref[...], NT)
    high, low = split(probes[:RANK] + probes[RANK : 2 * RANK] + probes[2 * RANK :])
    probe_ref[0] = jnp.concatenate([high] * GROUP, axis=0)
    probe_ref[1] = jnp.concatenate([low] * GROUP, axis=0)

    for k in [*range(1, n // 2), *range(n // 2, n)]:
        copies[k].wait_recv()
        block = flat_ref.at[core, slots_of(partner(owner, k, n))]
        shared.append(send(block, block, (cs, cr), k, device(0, 1)))
    for k in far_first:
        copies[k].wait_send()
    for copy in shared:
        copy.wait()

    order = list(range(chips - 1, 0, -1))
    sent = {}
    for g in range(groups):
        for k in order + [0]:
            step = there[k] * groups + g

            @pl.loop(0, GROUP)
            def _(q, step=step):
                a = slot_ref[(first_pair + step * GROUP + q) * 2]
                b = slot_ref[(first_pair + step * GROUP + q) * 2 + 1]
                for part in range(2):
                    left = flat_ref[part, a].astype(F32)
                    right = flat_ref[part, b].astype(F32)
                    lre, lim = left[:, :NF], left[:, NF:]
                    rre, rim = right[:, :NF], right[:, NF:]
                    at = pl.ds(pl.multiple_of((q * 2 + part) * win, 16), win)
                    cross_ref[step, at, :NF] = (lre * rre + lim * rim).astype(BF)
                    cross_ref[step, at, NF:] = (lim * rre - lre * rim).astype(BF)

            cross = cross_ref[step]
            probe = dot(probe_ref[0], cross, NT) + dot(probe_ref[1], cross, NT)
            high, low = split(jnp.where(own_block(lanes, RANK, rows, 2 * win), probe, 0.0))
            raw_buf[k, g] = (dot(high, cross) + dot(low, cross)).astype(BF)
            if k:
                sent[k, g] = send(
                    raw_buf.at[k, g], raw_in.at[k - 1, g], (rs, rr), (k - 1, g), device(k, 0)
                )
            wide = cross.astype(F32)
            energy = jnp.sum(wide * wide, axis=1, keepdims=True)
            energy = jnp.where(own_block(rows, 2 * win, lanes, RANK), energy, 0.0)
            energy_ref[step] = jnp.sum(energy, axis=0, keepdims=True)

    relay = chips == 4 and groups == 2
    loads[3].wait()
    raws, backs, given = [], [], {}
    for g in range(groups):
        raw = raw_buf[0, g].astype(F32)
        for k in order:
            sent[k, g].wait()
            raw = raw + raw_in[k - 1, g].astype(F32)
        high, low = split(raw)
        dual = dot(high, product_ref[0]) + (dot(high, product_ref[1]) + dot(low, product_ref[0]))
        back = eliminate(full(raw, dual, NT))
        dual_ref[0, g] = full(back, dual).astype(BF)
        for k in order:
            if not (relay and k == 3):
                given[k, g] = send(
                    dual_ref.at[0, g], dual_ref.at[k, g], (ds, dr), (k - 1, g), device(k, 0)
                )
        raws.append(raw)
        backs.append(back)

    def add_up(k, g):
        step = there[k] * groups + g
        coeffs = dot(cross_ref[step], dual_ref[k, g], NT)
        coeffs = jnp.where(own_block(rows, 2 * win, lanes, RANK), coeffs, 0.0)
        total = jnp.sum(coeffs, axis=0, keepdims=True)
        power = jnp.sum(coeffs * coeffs, axis=0, keepdims=True)
        pad = jnp.zeros((5, lanes), F32)
        sums_buf[k, g] = jnp.concatenate([total, power, energy_ref[step], pad], axis=0)

    summed = {}
    if relay:
        for g, via, to in ((0, 1, 2), (1, 2, 1)):
            given[via, g].wait()
            given[3, g] = send(
                dual_ref.at[via, g], dual_ref.at[3, g], (ds, dr), (2, g), device(to, 0)
            )
    else:
        for k in order:
            for g in range(groups):
                given[k, g].wait()
    for k in [0] + order[::-1]:
        for g in range(groups):
            if relay and k and (k, g) not in ((1, 0), (2, 1)):
                given[k, g].wait()
            add_up(k, g)
        if k:
            summed[k] = send(sums_buf.at[k], sums_in.at[k - 1], (ss, sr), k - 1, device(k, 0))
    sums = sums_buf[0]
    for k in order[::-1]:
        summed[k].wait()
        sums = sums + sums_in[k - 1]
    total, power, energy = sums[:, 0:1, :], sums[:, 1:2, :], sums[:, 2:3, :]
    weight = power / (power + energy / (2 * NF)) * total / windows
    mixed = []
    for g in range(groups):
        spread = jnp.where(own_block(GROUP, 1, lanes, RANK), weight[g], 0.0)
        mixed.append(full(full(spread, backs[g]), raws[g]))
    share_ref[core, me] = jnp.concatenate(mixed, axis=0).astype(share_ref.dtype)
    mine = share_ref.at[core, me]
    last = [send(mine, mine, (ws, wr), 2 * k + c - 1, device(k, c)) for k, c in everyone]
    for copy in last:
        copy.wait()

    weights = share_ref[...].reshape(PAIRS_DEV, 2 * NF)
    terms = [weights] if weights.dtype == BF else split(weights)
    for at in range(0, LAGS, 512):
        tile = inverse_ref[:, at : at + 512]
        out_ref[:, at : at + 512] = sum(dot(term, tile) for term in terms)


def pair_stacks(records, idx, slots, sketch, held, n, chips, windows):
    forward, inverse, product = held
    _, win, _ = records.shape
    pairs = slots.shape[0] // 4
    groups = pairs // chips // GROUP
    lanes = GROUP * RANK
    steps = pairs // GROUP
    own = pairs // chips
    vmem = pl.BlockSpec(memory_space=pltpu.VMEM)
    smem = pl.BlockSpec(memory_space=pltpu.SMEM)
    hbm = pl.BlockSpec(memory_space=pl.ANY)
    dma = pltpu.SemaphoreType.DMA
    return pl.pallas_call(
        functools.partial(kernel, n, chips, windows),
        in_specs=[smem, smem, vmem, hbm, hbm, hbm, hbm],
        out_specs=vmem,
        out_shape=jax.ShapeDtypeStruct((2 * pairs, LAGS), F32),
        scratch_shapes=[
            pltpu.VMEM(records.shape, BF),
            pltpu.VMEM(forward.shape, BF),
            pltpu.VMEM(inverse.shape, BF),
            pltpu.VMEM(product.shape, BF),
            pltpu.VMEM((2, chips, own, 2 * NF), BF if own % 16 == 0 else F32),
            pltpu.VMEM((n - 1, CAP, win, 2 * NF), BF),
            pltpu.VMEM((2, n * CAP, win, 2 * NF), BF),
            pltpu.VMEM((2, lanes, 2 * NF), BF),
            pltpu.VMEM((steps, GROUP * 2 * win, 2 * NF), BF),
            pltpu.VMEM((chips, groups, lanes, 2 * NF), BF),
            pltpu.VMEM((chips - 1, groups, lanes, 2 * NF), BF),
            pltpu.VMEM((steps, 1, lanes), F32),
            pltpu.VMEM((chips, groups, lanes, 2 * NF), BF),
            pltpu.VMEM((chips, groups, 8, lanes), F32),
            pltpu.VMEM((chips - 1, groups, 8, lanes), F32),
            dma((4,)),
            dma((n - 1,)),
            dma((n - 1,)),
            dma((n,)),
            dma((n,)),
            dma((chips - 1, groups)),
            dma((chips - 1, groups)),
            dma((chips - 1, groups)),
            dma((chips - 1, groups)),
            dma((chips - 1,)),
            dma((chips - 1,)),
            dma((2 * chips - 1,)),
            dma((2 * chips - 1,)),
        ],
        compiler_params=pltpu.CompilerParams(
            vmem_limit_bytes=VMEM, collective_id=0, has_side_effects=True
        ),
        name="pair_stacks",
    )(idx, slots, sketch, records, forward, inverse, product)


def plan(pair_list, n_pair, ch_dev, owner):
    lists = pair_list.reshape(n_pair, 2 * PAIRS_DEV)
    every = jnp.arange(n_pair * ch_dev)
    asked = jnp.any(lists[:, None, :] == every[None, :, None], axis=2)
    blocks = asked.reshape(n_pair, n_pair, ch_dev)
    before = jnp.arange(ch_dev)[None, :] < jnp.arange(ch_dev)[:, None]
    rank = jnp.sum((blocks[:, :, None, :] & before).astype(jnp.int32), axis=3)
    mine = lax.dynamic_slice_in_dim(blocks, owner, 1, 1)[:, 0]
    mine_rank = lax.dynamic_slice_in_dim(rank, owner, 1, 1)[:, 0]
    hit = mine[:, None, :] & (mine_rank[:, None, :] == jnp.arange(CAP)[None, :, None])
    idx = jnp.sum(jnp.where(hit, jnp.arange(ch_dev), 0), axis=2)
    place = (rank + CAP * jnp.arange(n_pair)[None, :, None]).reshape(n_pair, -1)
    place = lax.dynamic_slice_in_dim(place, owner, 1, 0)[0]
    wanted = lax.dynamic_slice_in_dim(lists, owner, 1, 0)[0]
    slots = jnp.sum(jnp.where(wanted[:, None] == every[None, :], place[None, :], 0), axis=1)
    return idx.astype(jnp.int32), slots.astype(jnp.int32)


def local(forward, inverse, product, records, pair_list, sketch):
    n_pair = lax.axis_size("pair")
    chips = lax.axis_size("chip")
    cores = lax.axis_size("core")
    owner = lax.axis_index("pair")
    ch_dev, win, _ = records.shape
    idx, slots = plan(pair_list, n_pair, ch_dev, owner)
    held = (forward, inverse, product)
    windows = win * chips * cores
    return pair_stacks(records, idx, slots, sketch, held, n_pair, chips, windows)


def solution(mesh):
    n_pair, n_tm = mesh.devices.shape
    fine = Mesh(mesh.devices.reshape(n_pair, n_tm // 2, 2), ("pair", "chip", "core"))
    forward, inverse, product = tables()
    in_specs = (P("pair", ("chip", "core"), None), P(), P())

    def run(records, pair_list, sketch):
        f = functools.partial(
            local, jnp.asarray(forward), jnp.asarray(inverse), jnp.asarray(product)
        )
        return jax.shard_map(
            f, mesh=fine, in_specs=in_specs, out_specs=P("pair", None), check_vma=False
        )(records, pair_list, sketch)

    return run
```
